32 devices in a mesh: sec: 2 (over x), cpl: 2 (over y), dom: 8 (over z, core).
Axes of the slice: x: 2, y: 2, z: 4, core: 2. Of those that a mesh axis runs over, the one named last changes fastest.
Arguments:
- component_fields: float32 [2, 24, 65536], P('sec', None, 'dom'), may hold values from -6 to 6
- wet_mask: int32 [2, 65536], P('sec', 'dom'), may hold values 0 or 1
- state_tiles: bfloat16 [2, 384, 128, 128], P('sec', ('cpl', 'dom')), may hold values from -0.625 to 0.625
- state_source: int32 [2, 384], P('sec', ('cpl', 'dom')), may hold values from 0 to 79
- state_target: int32 [2, 384], P('sec', ('cpl', 'dom')), may hold values from 0 to 63
- flux_tiles: bfloat16 [2, 384, 128, 128], P('sec', ('cpl', 'dom')), may hold values from -0.625 to 0.625
- flux_source: int32 [2, 384], P('sec', ('cpl', 'dom')), may hold values from 0 to 79
- flux_target: int32 [2, 384], P('sec', ('cpl', 'dom')), may hold values from 0 to 63
Outputs:
- delivered: float32 [2, 24, 65536], P('sec', None, 'dom')
- fluxes: float32 [2, 8, 65536], P('sec', None, 'dom')
The draws below stay inside these ranges and needn't reach their ends.
Inputs may be any that keep to these rules, and one draw needn't show every extreme that they name: `state_source`: a tile's source block counts the last 8 blocks of the dom index before the tile's own, then its own 64, then the first 8 of the one after, wrapping around. `flux_source`: as for state_source. `state_target`: a destination block among the 64 blocks of the other grid that share the tile's dom index. `flux_target`: as for state_target.
All inputs are finite; a program needn't handle non-finite values. No bound on the sum of `wet_mask` on one device may be relied on, other than what follows from the above.
Results may differ from the reference program's by a relative error of at most 0.0037.
Values may be sent and summed in bfloat16 or wider, within the bound.
A program may use at most 64 MiB of HBM per device.

```python
import jax
import jax.numpy as jnp
from jax import lax

F = 24
TILE = 128
BULK_ITERS = 3
RIM = 8
NBD = 64
TPD = 24
NCELL = 65536
NTILE = 384
N_CPL = 2
N_DOM = 8


def touch_ends(result, rng, least, top_value):
    shape = result.shape
    place = [jax.random.randint(jax.random.fold_in(rng, axis), (), 0, shape[axis]) for axis in range(len(shape))]
    result = result.at[tuple(place)].set(least)
    longest = shape.index(max(shape))
    place[longest] = (place[longest] + 1) % shape[longest]
    return result.at[tuple(place)].set(top_value)


def shard_levels(stream_key, extent, cuts, least, largest):
    gain, own = 1.0, jax.random.fold_in(stream_key, 6)
    for position, parts in cuts:
        heights = jnp.exp(jax.random.uniform(jax.random.fold_in(own, position), (parts,), jnp.float32, least / len(cuts), largest / len(cuts)))
        gain = gain * jnp.repeat(heights, extent[position] // parts).reshape([-1 if axis == position else 1 for axis in range(len(extent))])
    return gain


def bell_draw(rng, shape, deviation, bound, cuts=(), kind=jnp.bfloat16):
    array = deviation * jax.random.normal(rng, shape, jnp.float32)
    if cuts:
        array = array * shard_levels(rng, shape, cuts, -0.22, 0.18)
    return jnp.clip(array, -bound, bound).astype(kind)


def setup_inputs(seed: int = 0) -> dict:
    key_of = jax.random.split(jax.random.key(seed), 9)
    return {
        "component_fields": bell_draw(key_of[0], (2, F, NCELL), 1.0, 6.0, ((0, 2), (2, 8)), jnp.float32),
        "wet_mask": touch_ends((jax.random.randint(key_of[1], (2, NCELL), 0, 4) < 3).astype(jnp.int32), jax.random.fold_in(key_of[1], 1), 0, 1),
        "state_tiles": bell_draw(key_of[2], (2, NTILE, TILE, TILE), (TPD * N_CPL * TILE // NBD) ** -0.5, 0.625, ((0, 2), (1, 16))),
        "state_source": touch_ends(jax.random.randint(key_of[3], (2, NTILE), 0, NBD + 2 * RIM), jax.random.fold_in(key_of[3], 1), 0, (NBD + 2 * RIM) - 1).astype(jnp.int32),
        "state_target": touch_ends(jax.random.randint(key_of[4], (2, NTILE), 0, NBD), jax.random.fold_in(key_of[4], 1), 0, NBD - 1).astype(jnp.int32),
        "flux_tiles": bell_draw(key_of[5], (2, NTILE, TILE, TILE), (TPD * N_CPL * TILE // NBD) ** -0.5, 0.625, ((0, 2), (1, 16))),
        "flux_source": touch_ends(jax.random.randint(key_of[6], (2, NTILE), 0, NBD + 2 * RIM), jax.random.fold_in(key_of[6], 1), 0, (NBD + 2 * RIM) - 1).astype(jnp.int32),
        "flux_target": touch_ends(jax.random.randint(key_of[7], (2, NTILE), 0, NBD), jax.random.fold_in(key_of[7], 1), 0, NBD - 1).astype(jnp.int32),
    }


def remap_field(values_in, weights, source, target):
    row_count = values_in.shape[0]
    nblocks = NBD * N_DOM
    blocks = values_in.astype(jnp.bfloat16).reshape(row_count, nblocks, TILE)
    weights = weights.reshape(N_CPL * N_DOM, TPD, TILE, TILE)
    source = source.reshape(N_CPL * N_DOM, TPD).astype(jnp.int32)
    target = target.reshape(N_CPL * N_DOM, TPD).astype(jnp.int32)

    def one_holder(running, inputs):
        holder, tile_set, src_ix, dst_ix = inputs
        device = holder % N_DOM
        anchor = (device * NBD + src_ix - RIM) % nblocks
        finish = device * NBD + dst_ix
        pieces = blocks[:, anchor].astype(jnp.float32)
        product = jnp.einsum('rti,tij->rtj', pieces, tile_set.astype(jnp.float32))
        running = running.at[:, finish].add(product)
        return (running, None)
    init = jnp.zeros((row_count, nblocks, TILE), jnp.float32)
    holders = jnp.arange(N_CPL * N_DOM, dtype=jnp.int32)
    running, _ = lax.scan(one_holder, init, (holders, weights, source, target))
    return running.reshape(row_count, nblocks * TILE)

def bulk_flux(atmos, ocean, wet_frac):
    wind_u = atmos[0] - ocean[0]
    wind_v = atmos[1] - ocean[1]
    wind_speed = jnp.sqrt(wind_u * wind_u + wind_v * wind_v + 0.5)
    temp_diff = atmos[2] - ocean[2]
    humid_diff = atmos[3] - 0.5 * ocean[3]
    neutral = 1.0 + 0.5 * jnp.tanh(atmos[4] + ocean[4])
    richardson = 2.0 * temp_diff / (wind_speed * wind_speed)
    drag_coef = neutral
    for _ in range(BULK_ITERS):
        drag_coef = neutral * (1.0 + 0.8 * jnp.tanh(-richardson * drag_coef))
    transfer = drag_coef * wind_speed
    stacked = jnp.stack([0.5 * transfer * wind_u, 0.5 * transfer * wind_v, 0.5 * transfer * temp_diff, 0.5 * transfer * humid_diff, atmos[5] * (1.0 - 0.3 * jnp.tanh(ocean[5])), atmos[6] - 0.5 * ocean[2], atmos[7] - 0.15 * transfer * humid_diff, 0.5 * jnp.sqrt(drag_coef) * wind_speed])
    return stacked * wet_frac[None, :]

def reference(component_fields, wet_mask, state_tiles, state_source, state_target, flux_tiles, flux_source, flux_target):
    remapped = [remap_field(component_fields[section], state_tiles[section], state_source[section], state_target[section]) for section in range(2)]
    delivered = [remapped[1], remapped[0]]
    wet_frac = [wet_mask[section].astype(jnp.float32) for section in range(2)]
    flux_own = [bulk_flux(component_fields[0], delivered[0], wet_frac[0]), bulk_flux(delivered[1], component_fields[1], wet_frac[1])]
    sent_back = [remap_field(flux_own[section], flux_tiles[section], flux_source[section], flux_target[section]) for section in range(2)]
    merged = [0.5 * (flux_own[section] + wet_frac[section][None, :] * sent_back[1 - section]) for section in range(2)]
    return (jnp.stack(delivered), jnp.stack(merged))
```

```python
import functools

import jax
import jax.numpy as jnp
from jax import lax
from jax.experimental import pallas as pl
from jax.experimental.pallas import tpu as pltpu
from jax.sharding import PartitionSpec as P

TILE = 128
BULK_ITERS = 3
RIM = 8
CRIT = 8
MESH = pl.DeviceIdType.MESH


def bulk_flux(atmos, ocean, wet_frac):
    wind_u = atmos[0] - ocean[0]
    wind_v = atmos[1] - ocean[1]
    square = wind_u * wind_u + wind_v * wind_v + 0.5
    wind_speed = jnp.sqrt(square)
    temp_diff = atmos[2] - ocean[2]
    humid_diff = atmos[3] - 0.5 * ocean[3]
    neutral = 1.0 + 0.5 * jnp.tanh(atmos[4] + ocean[4])
    richardson = 2.0 * temp_diff / square
    drag_coef = neutral
    for _ in range(BULK_ITERS):
        drag_coef = neutral * (1.0 + 0.8 * jnp.tanh(-richardson * drag_coef))
    transfer = drag_coef * wind_speed
    rows = [
        0.5 * transfer * wind_u,
        0.5 * transfer * wind_v,
        0.5 * transfer * temp_diff,
        0.5 * transfer * humid_diff,
        atmos[5] * (1.0 - 0.3 * jnp.tanh(ocean[5])),
        atmos[6] - 0.5 * ocean[2],
        atmos[7] - 0.15 * transfer * humid_diff,
        0.5 * jnp.sqrt(drag_coef) * wind_speed,
    ]
    return [row * wet_frac for row in rows]


def kernel(
    sizes,
    ssrc, stgt, fsrc, ftgt,
    fields_hbm, wet_hbm, wstate_hbm, wflux_hbm,
    deliv_hbm, flux_hbm,
    xin, xext, wet, wstate, wflux, pcrit, prest, fbuf, fext, dout, fout, own_stage, got_stage,
    xsend, xrecv, fsend, frecv,
    tab, tab_recv, tab_own_s, tab_s,
    asend, arecv, bsend, brecv, csend, crecv, afull, cfull,
    load_sem, tabcopy_sem, out_sem,
    xs_sem, xr_sem, fs_sem, fr_sem,
    ts_sem, tr_sem, as_sem, ar_sem, bs_sem, br_sem, cs_sem, cr_sem,
):
    rows, nblk, tpd, ncpl, ndom = sizes
    rest = rows - CRIT
    edge = RIM * TILE
    cells = nblk * TILE
    sec = lax.axis_index("sec")
    cpl = lax.axis_index("cpl")
    dom = lax.axis_index("dom")
    right = lax.rem(dom + 1, ndom)
    left = lax.rem(dom + ndom - 1, ndom)
    other = 1 - sec

    loads = [
        pltpu.make_async_copy(fields_hbm.at[0, :, pl.ds(0, edge)], xin.at[:, pl.ds(0, edge)], load_sem.at[0]),
        pltpu.make_async_copy(fields_hbm.at[0, :, pl.ds(cells - edge, edge)], xin.at[:, pl.ds(cells - edge, edge)], load_sem.at[1]),
        pltpu.make_async_copy(fields_hbm.at[0, :, pl.ds(edge, cells - 2 * edge)], xin.at[:, pl.ds(edge, cells - 2 * edge)], load_sem.at[2]),
        pltpu.make_async_copy(wstate_hbm.at[0], wstate, load_sem.at[3]),
        pltpu.make_async_copy(wflux_hbm.at[0], wflux, load_sem.at[4]),
        pltpu.make_async_copy(wet_hbm, wet, load_sem.at[5]),
    ]
    for load in loads:
        load.start()

    barrier = pltpu.get_barrier_semaphore()
    for neighbour in (left, right):
        pl.semaphore_signal(barrier, inc=1, device_id={"dom": neighbour}, device_id_type=MESH)
    partners = [lax.rem(cpl + step, ncpl) for step in range(ncpl)]
    for partner in partners:
        pl.semaphore_signal(barrier, inc=1, device_id={"sec": other, "cpl": partner}, device_id_type=MESH)

    lane = lax.broadcasted_iota(jnp.int32, (8, 2 * nblk), 1)
    sub = lax.broadcasted_iota(jnp.int32, (8, 2 * nblk), 0)
    last = jnp.full((8, 2 * nblk), tpd, jnp.int32)
    prev = jnp.full((8, 2 * nblk), tpd, jnp.int32)
    trow = jnp.full((8, 2 * nblk), -1, jnp.int32)

    def mark(j, carry):
        last, trow = carry
        a = stgt[0, j]
        b = ftgt[0, j] + nblk
        last = jnp.where((lane == a) | (lane == b), j, last)
        trow = jnp.where(lane == j, a, trow)
        trow = jnp.where(lane == j + nblk, b, trow)
        return last, trow

    last, trow = lax.fori_loop(0, tpd, mark, (last, trow), unroll=True)

    def link(j, prev):
        a = stgt[0, j]
        b = ftgt[0, j] + nblk
        prev = jnp.where((trow == a) & (lane > j), j, prev)
        return jnp.where((trow == b) & (lane > j + nblk), j, prev)

    prev = lax.fori_loop(0, tpd, link, prev, unroll=True)
    tab[...] = jnp.where(sub == 0, last, prev)
    own_tab = pltpu.make_async_copy(tab, tab_own_s, tabcopy_sem.at[ncpl])
    own_tab.start()

    pcrit[tpd] = jnp.zeros((CRIT, TILE), jnp.float32)
    prest[tpd] = jnp.zeros((rest, TILE), jnp.float32)
    fbuf[tpd] = jnp.zeros((CRIT, TILE), jnp.float32)
    for k in range(ncpl):
        afull[k, tpd] = jnp.zeros((CRIT, TILE), jnp.float32)
        cfull[k, tpd] = jnp.zeros((CRIT, TILE), jnp.float32)
        brecv[k, tpd] = jnp.zeros((rest, TILE), jnp.bfloat16)

    for side in range(2):
        loads[side].wait()
        start = 0 if side == 0 else cells - edge
        for pair in range(RIM // 2):
            at = start + 2 * pair * TILE
            both = jnp.concatenate([xin[:, at : at + TILE], xin[:, at + TILE : at + 2 * TILE]], axis=0)
            xsend[side, 2 * rows * pair : 2 * rows * (pair + 1), :] = both.astype(jnp.bfloat16)

    pl.semaphore_wait(barrier, 2 + ncpl)

    def halo(send, recv, ssem, rsem, side):
        return pltpu.make_async_remote_copy(
            src_ref=send.at[side], dst_ref=recv.at[side], send_sem=ssem.at[side], recv_sem=rsem.at[side],
            device_id={"dom": left if side == 0 else right}, device_id_type=MESH,
        )

    def cross(src, dst, ssem, rsem, step):
        return pltpu.make_async_remote_copy(
            src_ref=src, dst_ref=dst(cpl), send_sem=ssem.at[step], recv_sem=rsem.at[cpl],
            device_id={"sec": other, "cpl": partners[step]}, device_id_type=MESH,
        )

    def arrived(src, dst, ssem, rsem, k):
        pltpu.make_async_remote_copy(
            src_ref=src, dst_ref=dst(k), send_sem=ssem.at[0], recv_sem=rsem.at[k],
            device_id={"sec": other}, device_id_type=MESH,
        ).wait_recv()

    xhalos = [halo(xsend, xrecv, xs_sem, xr_sem, side) for side in range(2)]
    for copy in xhalos:
        copy.start()
    tabs = [cross(tab, lambda k: tab_recv.at[k], ts_sem, tr_sem, step) for step in range(ncpl)]
    for copy in tabs:
        copy.start()

    own_tab.wait()
    loads[2].wait()

    def extend(group, carry):
        for i in range(8):
            b = group * 8 + i
            xext[RIM + b] = xin[:, pl.ds(pl.multiple_of(b * TILE, TILE), TILE)]
        return carry

    lax.fori_loop(0, nblk // 8, extend, 0)
    loads[3].wait()
    for side in range(2):
        xhalos[side].wait_recv()
        start = RIM + nblk if side == 0 else 0
        for pair in range(RIM // 2):
            at = start + 2 * pair
            both = xrecv[side, 2 * rows * pair : 2 * rows * (pair + 1), :].astype(jnp.float32)
            xext[at] = both[:rows]
            xext[at + 1] = both[rows:]

    def state_product(j, carry):
        piece = xext[ssrc[0, j]].astype(jnp.bfloat16)
        product = jnp.dot(piece, wstate[j], preferred_element_type=jnp.float32)
        pcrit[j] = product[:CRIT]
        prest[j] = product[CRIT:]
        return carry

    lax.fori_loop(0, tpd, state_product, 0, unroll=True)

    def chain_crit(j, carry):
        pcrit[j] = pcrit[j] + pcrit[tab_own_s[1, j]]
        return carry

    lax.fori_loop(0, tpd, chain_crit, 0, unroll=True)
    for pair in range(tpd // 2):
        both = jnp.concatenate([pcrit[2 * pair], pcrit[2 * pair + 1]], axis=0)
        asend[2 * CRIT * pair : 2 * CRIT * (pair + 1), :] = both.astype(jnp.bfloat16)
    acopies = [cross(asend, lambda k: arecv.at[k], as_sem, ar_sem, step) for step in range(ncpl)]
    for copy in reversed(acopies):
        copy.start()

    def chain_rest(j, carry):
        total = prest[j] + prest[tab_own_s[1, j]]
        prest[j] = total
        bsend[j] = total.astype(jnp.bfloat16)
        return carry

    lax.fori_loop(0, tpd, chain_rest, 0, unroll=True)
    bdst = lambda k: brecv.at[k, pl.ds(0, tpd)]
    bcopies = [cross(bsend, bdst, bs_sem, br_sem, step) for step in range(ncpl)]
    for copy in reversed(bcopies):
        copy.start()

    tabcopies = []
    for k in range(ncpl):
        arrived(tab, lambda k: tab_recv.at[k], ts_sem, tr_sem, k)
        copy = pltpu.make_async_copy(tab_recv.at[k], tab_s.at[k], tabcopy_sem.at[k])
        copy.start()
        tabcopies.append(copy)
    for copy in tabcopies:
        copy.wait()
    loads[5].wait()

    for k in range(ncpl):
        arrived(asend, lambda k: arecv.at[k], as_sem, ar_sem, k)
        for pair in range(tpd // 2):
            both = arecv[k, 2 * CRIT * pair : 2 * CRIT * (pair + 1), :].astype(jnp.float32)
            afull[k, 2 * pair] = both[:CRIT]
            afull[k, 2 * pair + 1] = both[CRIT:]

    first_sec = sec == 0

    def solve(group):
        for i in range(8):
            b = group * 8 + i
            got = afull[0, tab_s[0, 0, b]]
            for k in range(1, ncpl):
                got = got + afull[k, tab_s[k, 0, b]]
            at = pl.multiple_of(b * TILE, TILE)
            dout[:CRIT, pl.ds(at, TILE)] = got
            got_stage[CRIT * i : CRIT * (i + 1), :] = got
            own_stage[CRIT * i : CRIT * (i + 1), :] = xin[:CRIT, pl.ds(at, TILE)]
        atmos, ocean = [], []
        for r in range(CRIT):
            mine = own_stage[pl.ds(r, 8, stride=CRIT), :]
            got = got_stage[pl.ds(r, 8, stride=CRIT), :]
            atmos.append(jnp.where(first_sec, mine, got))
            ocean.append(jnp.where(first_sec, got, mine))
        wet_frac = wet[pl.ds(pl.multiple_of(group * 8, 8), 8), :].astype(jnp.float32)
        result = bulk_flux(atmos, ocean, wet_frac)
        for r in range(CRIT):
            got_stage[pl.ds(r, 8, stride=CRIT), :] = result[r]
        for i in range(8):
            fext[RIM + group * 8 + i] = got_stage[CRIT * i : CRIT * (i + 1), :]

    fhalos = [halo(fsend, frecv, fs_sem, fr_sem, side) for side in range(2)]
    for side, group in ((0, 0), (1, nblk // 8 - 1)):
        solve(group)
        fsend[side] = got_stage[...].astype(jnp.bfloat16)
        fhalos[side].start()

    def middle(group, carry):
        solve(group)
        return carry

    lax.fori_loop(1, nblk // 8 - 1, middle, 0)

    loads[4].wait()
    for side in range(2):
        fhalos[side].wait_recv()
        base = RIM + nblk if side == 0 else 0
        for pair in range(RIM // 2):
            both = frecv[side, 2 * CRIT * pair : 2 * CRIT * (pair + 1), :].astype(jnp.float32)
            fext[base + 2 * pair] = both[:CRIT]
            fext[base + 2 * pair + 1] = both[CRIT:]

    def flux_product(j, carry):
        piece = fext[fsrc[0, j]].astype(jnp.bfloat16)
        fbuf[j] = jnp.dot(piece, wflux[j], preferred_element_type=jnp.float32)
        return carry

    lax.fori_loop(0, tpd, flux_product, 0, unroll=True)

    def chain_flux(j, carry):
        fbuf[j] = fbuf[j] + fbuf[tab_own_s[1, j + nblk]]
        return carry

    lax.fori_loop(0, tpd, chain_flux, 0, unroll=True)
    for pair in range(tpd // 2):
        both = jnp.concatenate([fbuf[2 * pair], fbuf[2 * pair + 1]], axis=0)
        csend[2 * CRIT * pair : 2 * CRIT * (pair + 1), :] = both.astype(jnp.bfloat16)
    ccopies = [cross(csend, lambda k: crecv.at[k], cs_sem, cr_sem, step) for step in range(ncpl)]
    for copy in reversed(ccopies):
        copy.start()

    for k in range(ncpl):
        arrived(bsend, bdst, bs_sem, br_sem, k)

    def place(group, carry):
        for i in range(8):
            b = group * 8 + i
            got = brecv[0, tab_s[0, 0, b]].astype(jnp.float32)
            for k in range(1, ncpl):
                got = got + brecv[k, tab_s[k, 0, b]].astype(jnp.float32)
            dout[CRIT:, pl.ds(pl.multiple_of(b * TILE, TILE), TILE)] = got
        return carry

    lax.fori_loop(0, nblk // 8, place, 0)
    deliver = pltpu.make_async_copy(dout, deliv_hbm, out_sem.at[0])
    deliver.start()

    for k in range(ncpl):
        arrived(csend, lambda k: crecv.at[k], cs_sem, cr_sem, k)
        for pair in range(tpd // 2):
            both = crecv[k, 2 * CRIT * pair : 2 * CRIT * (pair + 1), :].astype(jnp.float32)
            cfull[k, 2 * pair] = both[:CRIT]
            cfull[k, 2 * pair + 1] = both[CRIT:]

    def merge(group, carry):
        wet_frac = wet[pl.ds(pl.multiple_of(group * 8, 8), 8), :].astype(jnp.float32)
        for i in range(8):
            b = group * 8 + i
            back = cfull[0, tab_s[0, 0, b + nblk]]
            for k in range(1, ncpl):
                back = back + cfull[k, tab_s[k, 0, b + nblk]]
            own = fext[RIM + b]
            fout[:, pl.ds(pl.multiple_of(b * TILE, TILE), TILE)] = 0.5 * (own + wet_frac[i : i + 1] * back)
        return carry

    lax.fori_loop(0, nblk // 8, merge, 0)
    store = pltpu.make_async_copy(fout, flux_hbm, out_sem.at[1])
    store.start()

    for copy in xhalos + tabs + acopies + bcopies + fhalos + ccopies:
        copy.wait_send()
    deliver.wait()
    store.wait()


def body(ncpl, ndom, fields, wet_mask, wstate, ssrc, stgt, wflux, fsrc, ftgt):
    rows, cells = fields.shape[1:]
    nblk = cells // TILE
    tpd = wstate.shape[1]
    rest = rows - CRIT
    f32, bf16, i32 = jnp.float32, jnp.bfloat16, jnp.int32
    vmem, dma = pltpu.VMEM, pltpu.SemaphoreType.DMA
    smem_spec = pl.BlockSpec(memory_space=pltpu.SMEM)
    any_spec = pl.BlockSpec(memory_space=pl.ANY)
    delivered, fluxes = pl.pallas_call(
        functools.partial(kernel, (rows, nblk, tpd, ncpl, ndom)),
        out_shape=(
            jax.ShapeDtypeStruct((rows, cells), f32),
            jax.ShapeDtypeStruct((CRIT, cells), f32),
        ),
        in_specs=[smem_spec] * 4 + [any_spec] * 4,
        out_specs=(any_spec, any_spec),
        scratch_shapes=[
            vmem((rows, cells), f32),
            vmem((nblk + 2 * RIM, rows, TILE), f32),
            vmem((nblk, TILE), i32),
            vmem((tpd, TILE, TILE), bf16),
            vmem((tpd, TILE, TILE), bf16),
            vmem((tpd + 1, CRIT, TILE), f32),
            vmem((tpd + 1, rest, TILE), f32),
            vmem((tpd + 1, CRIT, TILE), f32),
            vmem((nblk + 2 * RIM, CRIT, TILE), f32),
            vmem((rows, cells), f32),
            vmem((CRIT, cells), f32),
            vmem((8 * CRIT, TILE), f32),
            vmem((8 * CRIT, TILE), f32),
            vmem((2, RIM * rows, TILE), bf16),
            vmem((2, RIM * rows, TILE), bf16),
            vmem((2, RIM * CRIT, TILE), bf16),
            vmem((2, RIM * CRIT, TILE), bf16),
            vmem((8, 2 * nblk), i32),
            vmem((ncpl, 8, 2 * nblk), i32),
            pltpu.SMEM((8, 2 * nblk), i32),
            pltpu.SMEM((ncpl, 8, 2 * nblk), i32),
            vmem((tpd * CRIT, TILE), bf16),
            vmem((ncpl, tpd * CRIT, TILE), bf16),
            vmem((tpd, rest, TILE), bf16),
            vmem((ncpl, tpd + 1, rest, TILE), bf16),
            vmem((tpd * CRIT, TILE), bf16),
            vmem((ncpl, tpd * CRIT, TILE), bf16),
            vmem((ncpl, tpd + 1, CRIT, TILE), f32),
            vmem((ncpl, tpd + 1, CRIT, TILE), f32),
            dma((6,)), dma((ncpl + 1,)), dma((2,)),
            dma((2,)), dma((2,)), dma((2,)), dma((2,)),
            dma((ncpl,)), dma((ncpl,)), dma((ncpl,)), dma((ncpl,)),
            dma((ncpl,)), dma((ncpl,)), dma((ncpl,)), dma((ncpl,)),
        ],
        compiler_params=pltpu.CompilerParams(
            collective_id=0, has_side_effects=True, vmem_limit_bytes=40 * 1024 * 1024
        ),
    )(ssrc, stgt, fsrc, ftgt, fields, wet_mask.reshape(nblk, TILE), wstate, wflux)
    return delivered[None], fluxes[None]


def solution(mesh):
    tile_spec = P("sec", ("cpl", "dom"), None, None)
    index_spec = P("sec", ("cpl", "dom"))
    return jax.shard_map(
        functools.partial(body, mesh.shape["cpl"], mesh.shape["dom"]),
        mesh=mesh,
        in_specs=(
            P("sec", None, "dom"), P("sec", "dom"),
            tile_spec, index_spec, index_spec,
            tile_spec, index_spec, index_spec,
        ),
        out_specs=(P("sec", None, "dom"), P("sec", None, "dom")),
        check_vma=False,
    )
```

```python
import functools

import jax
import jax.numpy as jnp
from jax import lax
from jax.experimental import pallas as pl
from jax.experimental.pallas import tpu as pltpu
from jax.sharding import PartitionSpec as P

TILE = 128
BULK_ITERS = 3
RIM = 8
CRIT = 8
MESH = pl.DeviceIdType.MESH


def bulk_flux(atmos, ocean, wet_frac):
    wind_u = atmos[0] - ocean[0]
    wind_v = atmos[1] - ocean[1]
    square = wind_u * wind_u + wind_v * wind_v + 0.5
    wind_speed = jnp.sqrt(square)
    temp_diff = atmos[2] - ocean[2]
    humid_diff = atmos[3] - 0.5 * ocean[3]
    neutral = 1.0 + 0.5 * jnp.tanh(atmos[4] + ocean[4])
    richardson = 2.0 * temp_diff / square
    drag_coef = neutral
    for _ in range(BULK_ITERS):
        drag_coef = neutral * (1.0 + 0.8 * jnp.tanh(-richardson * drag_coef))
    transfer = drag_coef * wind_speed
    rows = [
        0.5 * transfer * wind_u,
        0.5 * transfer * wind_v,
        0.5 * transfer * temp_diff,
        0.5 * transfer * humid_diff,
        atmos[5] * (1.0 - 0.3 * jnp.tanh(ocean[5])),
        atmos[6] - 0.5 * ocean[2],
        atmos[7] - 0.15 * transfer * humid_diff,
        0.5 * jnp.sqrt(drag_coef) * wind_speed,
    ]
    return [row * wet_frac for row in rows]


def kernel(
    sizes,
    ssrc_hbm, stgt_hbm, fsrc_hbm, ftgt_hbm,
    fields_hbm, wet_hbm, wstate_hbm, wflux_hbm,
    deliv_hbm, flux_hbm,
    ssrc, stgt, fsrc, ftgt,
    xin, xext, wet, wstate, wflux, pcrit, prest, fbuf, fext, dout, fout, own_stage, got_stage,
    xsend, xrecv, fsend, frecv,
    tab, tab_recv, tab_own_s, tab_s,
    asend, arecv, bsend, brecv, csend, crecv, afull, cfull,
    load_sem, tabcopy_sem, out_sem,
    xs_sem, xr_sem, fs_sem, fr_sem,
    ts_sem, tr_sem, as_sem, ar_sem, bs_sem, br_sem, cs_sem, cr_sem,
):
    rows, nblk, tpd, ncpl, ndom = sizes
    rest = rows - CRIT
    edge = RIM * TILE
    cells = nblk * TILE
    sec = lax.axis_index("sec")
    cpl = lax.axis_index("cpl")
    dom = lax.axis_index("dom")
    right = lax.rem(dom + 1, ndom)
    left = lax.rem(dom + ndom - 1, ndom)
    other = 1 - sec

    indices = [
        pltpu.make_async_copy(src, dst, load_sem.at[6 + i])
        for i, (src, dst) in enumerate(((stgt_hbm, stgt), (ftgt_hbm, ftgt), (ssrc_hbm, ssrc), (fsrc_hbm, fsrc)))
    ]
    for load in indices:
        load.start()
    loads = [
        pltpu.make_async_copy(fields_hbm.at[0, :, pl.ds(0, edge)], xin.at[:, pl.ds(0, edge)], load_sem.at[0]),
        pltpu.make_async_copy(fields_hbm.at[0, :, pl.ds(cells - edge, edge)], xin.at[:, pl.ds(cells - edge, edge)], load_sem.at[1]),
        pltpu.make_async_copy(fields_hbm.at[0, :, pl.ds(edge, cells - 2 * edge)], xin.at[:, pl.ds(edge, cells - 2 * edge)], load_sem.at[2]),
        pltpu.make_async_copy(wstate_hbm.at[0], wstate, load_sem.at[3]),
        pltpu.make_async_copy(wflux_hbm.at[0], wflux, load_sem.at[4]),
        pltpu.make_async_copy(wet_hbm, wet, load_sem.at[5]),
    ]
    for load in loads:
        load.start()

    barrier = pltpu.get_barrier_semaphore()
    for neighbour in (left, right):
        pl.semaphore_signal(barrier, inc=1, device_id={"dom": neighbour}, device_id_type=MESH)
    partners = [lax.rem(cpl + step, ncpl) for step in range(ncpl)]
    for partner in partners:
        pl.semaphore_signal(barrier, inc=1, device_id={"sec": other, "cpl": partner}, device_id_type=MESH)

    lane = lax.broadcasted_iota(jnp.int32, (8, 2 * nblk), 1)
    sub = lax.broadcasted_iota(jnp.int32, (8, 2 * nblk), 0)
    last = jnp.full((8, 2 * nblk), tpd, jnp.int32)
    prev = jnp.full((8, 2 * nblk), tpd, jnp.int32)
    trow = jnp.full((8, 2 * nblk), -1, jnp.int32)

    for load in indices:
        load.wait()

    def mark(j, carry):
        last, trow = carry
        a = stgt[0, j]
        b = ftgt[0, j] + nblk
        last = jnp.where((lane == a) | (lane == b), j, last)
        trow = jnp.where(lane == j, a, trow)
        trow = jnp.where(lane == j + nblk, b, trow)
        return last, trow

    last, trow = lax.fori_loop(0, tpd, mark, (last, trow), unroll=True)

    def link(j, prev):
        a = stgt[0, j]
        b = ftgt[0, j] + nblk
        prev = jnp.where((trow == a) & (lane > j), j, prev)
        return jnp.where((trow == b) & (lane > j + nblk), j, prev)

    prev = lax.fori_loop(0, tpd, link, prev, unroll=True)
    tab[...] = jnp.where(sub == 0, last, prev)
    own_tab = pltpu.make_async_copy(tab, tab_own_s, tabcopy_sem.at[ncpl])
    own_tab.start()

    pcrit[tpd] = jnp.zeros((CRIT, TILE), jnp.float32)
    prest[tpd] = jnp.zeros((rest, TILE), jnp.float32)
    fbuf[tpd] = jnp.zeros((CRIT, TILE), jnp.float32)
    for k in range(ncpl):
        afull[k, tpd] = jnp.zeros((CRIT, TILE), jnp.float32)
        cfull[k, tpd] = jnp.zeros((CRIT, TILE), jnp.float32)
        brecv[k, tpd] = jnp.zeros((rest, TILE), jnp.bfloat16)

    for side in range(2):
        loads[side].wait()
        start = 0 if side == 0 else cells - edge
        for pair in range(RIM // 2):
            at = start + 2 * pair * TILE
            both = jnp.concatenate([xin[:, at : at + TILE], xin[:, at + TILE : at + 2 * TILE]], axis=0)
            xsend[side, 2 * rows * pair : 2 * rows * (pair + 1), :] = both.astype(jnp.bfloat16)

    pl.semaphore_wait(barrier, 2 + ncpl)

    def halo(send, recv, ssem, rsem, side):
        return pltpu.make_async_remote_copy(
            src_ref=send.at[side], dst_ref=recv.at[side], send_sem=ssem.at[side], recv_sem=rsem.at[side],
            device_id={"dom": left if side == 0 else right}, device_id_type=MESH,
        )

    def cross(src, dst, ssem, rsem, step):
        return pltpu.make_async_remote_copy(
            src_ref=src, dst_ref=dst(cpl), send_sem=ssem.at[step], recv_sem=rsem.at[cpl],
            device_id={"sec": other, "cpl": partners[step]}, device_id_type=MESH,
        )

    def arrived(src, dst, ssem, rsem, k):
        pltpu.make_async_remote_copy(
            src_ref=src, dst_ref=dst(k), send_sem=ssem.at[0], recv_sem=rsem.at[k],
            device_id={"sec": other}, device_id_type=MESH,
        ).wait_recv()

    xhalos = [halo(xsend, xrecv, xs_sem, xr_sem, side) for side in range(2)]
    for copy in xhalos:
        copy.start()
    tabs = [cross(tab, lambda k: tab_recv.at[k], ts_sem, tr_sem, step) for step in range(ncpl)]
    for copy in tabs:
        copy.start()

    own_tab.wait()
    loads[2].wait()

    def extend(group, carry):
        for i in range(8):
            b = group * 8 + i
            xext[RIM + b] = xin[:, pl.ds(pl.multiple_of(b * TILE, TILE), TILE)]
        return carry

    lax.fori_loop(0, nblk // 8, extend, 0)
    loads[3].wait()
    for side in range(2):
        xhalos[side].wait_recv()
        start = RIM + nblk if side == 0 else 0
        for pair in range(RIM // 2):
            at = start + 2 * pair
            both = xrecv[side, 2 * rows * pair : 2 * rows * (pair + 1), :].astype(jnp.float32)
            xext[at] = both[:rows]
            xext[at + 1] = both[rows:]

    def state_product(j, carry):
        piece = xext[ssrc[0, j]].astype(jnp.bfloat16)
        product = jnp.dot(piece, wstate[j], preferred_element_type=jnp.float32)
        pcrit[j] = product[:CRIT]
        prest[j] = product[CRIT:]
        return carry

    lax.fori_loop(0, tpd, state_product, 0, unroll=True)

    def chain_crit(j, carry):
        pcrit[j] = pcrit[j] + pcrit[tab_own_s[1, j]]
        return carry

    lax.fori_loop(0, tpd, chain_crit, 0, unroll=True)
    for pair in range(tpd // 2):
        both = jnp.concatenate([pcrit[2 * pair], pcrit[2 * pair + 1]], axis=0)
        asend[2 * CRIT * pair : 2 * CRIT * (pair + 1), :] = both.astype(jnp.bfloat16)
    acopies = [cross(asend, lambda k: arecv.at[k], as_sem, ar_sem, step) for step in range(ncpl)]
    for copy in reversed(acopies):
        copy.start()

    def chain_rest(j, carry):
        total = prest[j] + prest[tab_own_s[1, j]]
        prest[j] = total
        bsend[j] = total.astype(jnp.bfloat16)
        return carry

    lax.fori_loop(0, tpd, chain_rest, 0, unroll=True)
    bdst = lambda k: brecv.at[k, pl.ds(0, tpd)]
    bcopies = [cross(bsend, bdst, bs_sem, br_sem, step) for step in range(ncpl)]
    for copy in reversed(bcopies):
        copy.start()

    tabcopies = []
    for k in range(ncpl):
        arrived(tab, lambda k: tab_recv.at[k], ts_sem, tr_sem, k)
        copy = pltpu.make_async_copy(tab_recv.at[k], tab_s.at[k], tabcopy_sem.at[k])
        copy.start()
        tabcopies.append(copy)
    for copy in tabcopies:
        copy.wait()
    loads[5].wait()

    for k in range(ncpl):
        arrived(asend, lambda k: arecv.at[k], as_sem, ar_sem, k)
        for pair in range(tpd // 2):
            both = arecv[k, 2 * CRIT * pair : 2 * CRIT * (pair + 1), :].astype(jnp.float32)
            afull[k, 2 * pair] = both[:CRIT]
            afull[k, 2 * pair + 1] = both[CRIT:]

    first_sec = sec == 0

    def solve(group):
        for i in range(8):
            b = group * 8 + i
            got = afull[0, tab_s[0, 0, b]]
            for k in range(1, ncpl):
                got = got + afull[k, tab_s[k, 0, b]]
            at = pl.multiple_of(b * TILE, TILE)
            dout[:CRIT, pl.ds(at, TILE)] = got
            got_stage[CRIT * i : CRIT * (i + 1), :] = got
            own_stage[CRIT * i : CRIT * (i + 1), :] = xin[:CRIT, pl.ds(at, TILE)]
        atmos, ocean = [], []
        for r in range(CRIT):
            mine = own_stage[pl.ds(r, 8, stride=CRIT), :]
            got = got_stage[pl.ds(r, 8, stride=CRIT), :]
            atmos.append(jnp.where(first_sec, mine, got))
            ocean.append(jnp.where(first_sec, got, mine))
        wet_frac = wet[pl.ds(pl.multiple_of(group * 8, 8), 8), :].astype(jnp.float32)
        result = bulk_flux(atmos, ocean, wet_frac)
        for r in range(CRIT):
            got_stage[pl.ds(r, 8, stride=CRIT), :] = result[r]
        for i in range(8):
            fext[RIM + group * 8 + i] = got_stage[CRIT * i : CRIT * (i + 1), :]

    fhalos = [halo(fsend, frecv, fs_sem, fr_sem, side) for side in range(2)]
    for side, group in ((0, 0), (1, nblk // 8 - 1)):
        solve(group)
        fsend[side] = got_stage[...].astype(jnp.bfloat16)
        fhalos[side].start()

    def middle(group, carry):
        solve(group)
        return carry

    lax.fori_loop(1, nblk // 8 - 1, middle, 0)

    loads[4].wait()
    for side in range(2):
        fhalos[side].wait_recv()
        base = RIM + nblk if side == 0 else 0
        for pair in range(RIM // 2):
            both = frecv[side, 2 * CRIT * pair : 2 * CRIT * (pair + 1), :].astype(jnp.float32)
            fext[base + 2 * pair] = both[:CRIT]
            fext[base + 2 * pair + 1] = both[CRIT:]

    def flux_product(j, carry):
        piece = fext[fsrc[0, j]].astype(jnp.bfloat16)
        fbuf[j] = jnp.dot(piece, wflux[j], preferred_element_type=jnp.float32)
        return carry

    lax.fori_loop(0, tpd, flux_product, 0, unroll=True)

    def chain_flux(j, carry):
        fbuf[j] = fbuf[j] + fbuf[tab_own_s[1, j + nblk]]
        return carry

    lax.fori_loop(0, tpd, chain_flux, 0, unroll=True)
    for pair in range(tpd // 2):
        both = jnp.concatenate([fbuf[2 * pair], fbuf[2 * pair + 1]], axis=0)
        csend[2 * CRIT * pair : 2 * CRIT * (pair + 1), :] = both.astype(jnp.bfloat16)
    ccopies = [cross(csend, lambda k: crecv.at[k], cs_sem, cr_sem, step) for step in range(ncpl)]
    for copy in reversed(ccopies):
        copy.start()

    for k in range(ncpl):
        arrived(bsend, bdst, bs_sem, br_sem, k)

    def place(group, carry):
        for i in range(8):
            b = group * 8 + i
            got = brecv[0, tab_s[0, 0, b]].astype(jnp.float32)
            for k in range(1, ncpl):
                got = got + brecv[k, tab_s[k, 0, b]].astype(jnp.float32)
            dout[CRIT:, pl.ds(pl.multiple_of(b * TILE, TILE), TILE)] = got
        return carry

    lax.fori_loop(0, nblk // 8, place, 0)
    deliver = pltpu.make_async_copy(dout, deliv_hbm, out_sem.at[0])
    deliver.start()

    for k in range(ncpl):
        arrived(csend, lambda k: crecv.at[k], cs_sem, cr_sem, k)
        for pair in range(tpd // 2):
            both = crecv[k, 2 * CRIT * pair : 2 * CRIT * (pair + 1), :].astype(jnp.float32)
            cfull[k, 2 * pair] = both[:CRIT]
            cfull[k, 2 * pair + 1] = both[CRIT:]

    def merge(group, carry):
        wet_frac = wet[pl.ds(pl.multiple_of(group * 8, 8), 8), :].astype(jnp.float32)
        for i in range(8):
            b = group * 8 + i
            back = cfull[0, tab_s[0, 0, b + nblk]]
            for k in range(1, ncpl):
                back = back + cfull[k, tab_s[k, 0, b + nblk]]
            own = fext[RIM + b]
            fout[:, pl.ds(pl.multiple_of(b * TILE, TILE), TILE)] = 0.5 * (own + wet_frac[i : i + 1] * back)
        return carry

    lax.fori_loop(0, nblk // 8, merge, 0)
    store = pltpu.make_async_copy(fout, flux_hbm, out_sem.at[1])
    store.start()

    for copy in xhalos + tabs + acopies + bcopies + fhalos + ccopies:
        copy.wait_send()
    deliver.wait()
    store.wait()


def body(ncpl, ndom, fields, wet_mask, wstate, ssrc, stgt, wflux, fsrc, ftgt):
    rows, cells = fields.shape[1:]
    nblk = cells // TILE
    tpd = wstate.shape[1]
    rest = rows - CRIT
    f32, bf16, i32 = jnp.float32, jnp.bfloat16, jnp.int32
    vmem, dma = pltpu.VMEM, pltpu.SemaphoreType.DMA
    hbm_spec = pl.BlockSpec(memory_space=pltpu.HBM)
    delivered, fluxes = pl.pallas_call(
        functools.partial(kernel, (rows, nblk, tpd, ncpl, ndom)),
        out_shape=(
            jax.ShapeDtypeStruct((rows, cells), f32),
            jax.ShapeDtypeStruct((CRIT, cells), f32),
        ),
        in_specs=[hbm_spec] * 8,
        out_specs=(hbm_spec, hbm_spec),
        scratch_shapes=[pltpu.SMEM((1, tpd), i32)] * 4
        + [
            vmem((rows, cells), f32),
            vmem((nblk + 2 * RIM, rows, TILE), f32),
            vmem((nblk, TILE), i32),
            vmem((tpd, TILE, TILE), bf16),
            vmem((tpd, TILE, TILE), bf16),
            vmem((tpd + 1, CRIT, TILE), f32),
            vmem((tpd + 1, rest, TILE), f32),
            vmem((tpd + 1, CRIT, TILE), f32),
            vmem((nblk + 2 * RIM, CRIT, TILE), f32),
            vmem((rows, cells), f32),
            vmem((CRIT, cells), f32),
            vmem((8 * CRIT, TILE), f32),
            vmem((8 * CRIT, TILE), f32),
            vmem((2, RIM * rows, TILE), bf16),
            vmem((2, RIM * rows, TILE), bf16),
            vmem((2, RIM * CRIT, TILE), bf16),
            vmem((2, RIM * CRIT, TILE), bf16),
            vmem((8, 2 * nblk), i32),
            vmem((ncpl, 8, 2 * nblk), i32),
            pltpu.SMEM((8, 2 * nblk), i32),
            pltpu.SMEM((ncpl, 8, 2 * nblk), i32),
            vmem((tpd * CRIT, TILE), bf16),
            vmem((ncpl, tpd * CRIT, TILE), bf16),
            vmem((tpd, rest, TILE), bf16),
            vmem((ncpl, tpd + 1, rest, TILE), bf16),
            vmem((tpd * CRIT, TILE), bf16),
            vmem((ncpl, tpd * CRIT, TILE), bf16),
            vmem((ncpl, tpd + 1, CRIT, TILE), f32),
            vmem((ncpl, tpd + 1, CRIT, TILE), f32),
            dma((10,)), dma((ncpl + 1,)), dma((2,)),
            dma((2,)), dma((2,)), dma((2,)), dma((2,)),
            dma((ncpl,)), dma((ncpl,)), dma((ncpl,)), dma((ncpl,)),
            dma((ncpl,)), dma((ncpl,)), dma((ncpl,)), dma((ncpl,)),
        ],
        compiler_params=pltpu.CompilerParams(
            collective_id=0, has_side_effects=True, vmem_limit_bytes=63 * 1024 * 1024
        ),
    )(ssrc, stgt, fsrc, ftgt, fields, wet_mask.reshape(nblk, TILE), wstate, wflux)
    return delivered[None], fluxes[None]


def solution(mesh):
    tile_spec = P("sec", ("cpl", "dom"), None, None)
    index_spec = P("sec", ("cpl", "dom"))
    return jax.shard_map(
        functools.partial(body, mesh.shape["cpl"], mesh.shape["dom"]),
        mesh=mesh,
        in_specs=(
            P("sec", None, "dom"), P("sec", "dom"),
            tile_spec, index_spec, index_spec,
            tile_spec, index_spec, index_spec,
        ),
        out_specs=(P("sec", None, "dom"), P("sec", None, "dom")),
        check_vma=False,
    )
```

```python
import functools

import jax
import jax.numpy as jnp
from jax import lax
from jax.experimental import pallas as pl
from jax.experimental.pallas import tpu as pltpu
from jax.sharding import PartitionSpec as P

TILE = 128
BULK_ITERS = 3
RIM = 8
CRIT = 8
MESH = pl.DeviceIdType.MESH


def bulk_flux(atmos, ocean, wet_frac):
    wind_u = atmos[0] - ocean[0]
    wind_v = atmos[1] - ocean[1]
    square = wind_u * wind_u + wind_v * wind_v + 0.5
    wind_speed = jnp.sqrt(square)
    temp_diff = atmos[2] - ocean[2]
    humid_diff = atmos[3] - 0.5 * ocean[3]
    neutral = 1.0 + 0.5 * jnp.tanh(atmos[4] + ocean[4])
    richardson = 2.0 * temp_diff / square
    drag_coef = neutral
    for _ in range(BULK_ITERS):
        drag_coef = neutral * (1.0 + 0.8 * jnp.tanh(-richardson * drag_coef))
    transfer = drag_coef * wind_speed
    rows = [
        0.5 * transfer * wind_u,
        0.5 * transfer * wind_v,
        0.5 * transfer * temp_diff,
        0.5 * transfer * humid_diff,
        atmos[5] * (1.0 - 0.3 * jnp.tanh(ocean[5])),
        atmos[6] - 0.5 * ocean[2],
        atmos[7] - 0.15 * transfer * humid_diff,
        0.5 * jnp.sqrt(drag_coef) * wind_speed,
    ]
    return [row * wet_frac for row in rows]


def kernel(
    sizes,
    ssrc_hbm, stgt_hbm, fsrc_hbm, ftgt_hbm,
    fields_hbm, wet_hbm, wstate_hbm, wflux_hbm,
    deliv_hbm, flux_hbm,
    ssrc, stgt, fsrc, ftgt,
    xin, xcrit, xrest, wet, wstate, wflux, pcrit, prest, fbuf, fext, dout, fout, own_stage, got_stage,
    xsend, xrecv, fsend, frecv,
    tab, tab_recv, tab_own_s, tab_s,
    asend, arecv, bsend, brecv, csend, crecv, afull, cfull,
    load_sem, tabcopy_sem, out_sem,
    xs_sem, xr_sem, ys_sem, yr_sem, fs_sem, fr_sem,
    ts_sem, tr_sem, as_sem, ar_sem, bs_sem, br_sem, cs_sem, cr_sem,
):
    rows, nblk, tpd, ncpl, ndom = sizes
    rest = rows - CRIT
    edge = RIM * TILE
    cells = nblk * TILE
    sec = lax.axis_index("sec")
    cpl = lax.axis_index("cpl")
    dom = lax.axis_index("dom")
    right = lax.rem(dom + 1, ndom)
    left = lax.rem(dom + ndom - 1, ndom)
    other = 1 - sec

    indices = [
        pltpu.make_async_copy(src, dst, load_sem.at[6 + i])
        for i, (src, dst) in enumerate(((stgt_hbm, stgt), (ftgt_hbm, ftgt), (ssrc_hbm, ssrc), (fsrc_hbm, fsrc)))
    ]
    for load in indices:
        load.start()
    loads = [
        pltpu.make_async_copy(fields_hbm.at[0, :, pl.ds(0, edge)], xin.at[:, pl.ds(0, edge)], load_sem.at[0]),
        pltpu.make_async_copy(fields_hbm.at[0, :, pl.ds(cells - edge, edge)], xin.at[:, pl.ds(cells - edge, edge)], load_sem.at[1]),
        pltpu.make_async_copy(fields_hbm.at[0, :, pl.ds(edge, cells - 2 * edge)], xin.at[:, pl.ds(edge, cells - 2 * edge)], load_sem.at[2]),
        pltpu.make_async_copy(wstate_hbm.at[0], wstate, load_sem.at[3]),
        pltpu.make_async_copy(wflux_hbm.at[0], wflux, load_sem.at[4]),
        pltpu.make_async_copy(wet_hbm, wet, load_sem.at[5]),
    ]
    for load in loads:
        load.start()

    barrier = pltpu.get_barrier_semaphore()
    for neighbour in (left, right):
        pl.semaphore_signal(barrier, inc=1, device_id={"dom": neighbour}, device_id_type=MESH)
    partners = [lax.rem(cpl + step, ncpl) for step in range(ncpl)]
    for partner in partners:
        pl.semaphore_signal(barrier, inc=1, device_id={"sec": other, "cpl": partner}, device_id_type=MESH)
    for partner in partners[1:]:
        pl.semaphore_signal(barrier, inc=1, device_id={"cpl": partner}, device_id_type=MESH)

    lane = lax.broadcasted_iota(jnp.int32, (8, 2 * nblk), 1)
    sub = lax.broadcasted_iota(jnp.int32, (8, 2 * nblk), 0)
    last = jnp.full((8, 2 * nblk), tpd, jnp.int32)
    prev = jnp.full((8, 2 * nblk), tpd, jnp.int32)
    trow = jnp.full((8, 2 * nblk), -1, jnp.int32)

    for load in indices:
        load.wait()

    def mark(j, carry):
        last, trow = carry
        a = stgt[0, j]
        b = ftgt[0, j] + nblk
        last = jnp.where((lane == a) | (lane == b), j, last)
        trow = jnp.where(lane == j, a, trow)
        trow = jnp.where(lane == j + nblk, b, trow)
        return last, trow

    last, trow = lax.fori_loop(0, tpd, mark, (last, trow), unroll=True)

    def link(j, prev):
        a = stgt[0, j]
        b = ftgt[0, j] + nblk
        prev = jnp.where((trow == a) & (lane > j), j, prev)
        return jnp.where((trow == b) & (lane > j + nblk), j, prev)

    prev = lax.fori_loop(0, tpd, link, prev, unroll=True)
    tab[...] = jnp.where(sub == 0, last, prev)
    own_tab = pltpu.make_async_copy(tab, tab_own_s, tabcopy_sem.at[ncpl])
    own_tab.start()

    pcrit[tpd] = jnp.zeros((CRIT, TILE), jnp.float32)
    prest[tpd] = jnp.zeros((rest, TILE), jnp.float32)
    fbuf[tpd] = jnp.zeros((CRIT, TILE), jnp.float32)
    for k in range(ncpl):
        afull[k, tpd] = jnp.zeros((CRIT, TILE), jnp.float32)
        cfull[k, tpd] = jnp.zeros((CRIT, TILE), jnp.float32)
        brecv[k, tpd] = jnp.zeros((rest, TILE), jnp.bfloat16)

    def extend(b):
        at = b * TILE if isinstance(b, int) else pl.multiple_of(b * TILE, TILE)
        xcrit[RIM + b] = xin[:CRIT, pl.ds(at, TILE)]
        xrest[RIM + b] = xin[CRIT:, pl.ds(at, TILE)].astype(jnp.bfloat16)

    def pack(send, side, ext, start):
        for pair in range(RIM // 2):
            both = jnp.concatenate([ext[start + 2 * pair], ext[start + 2 * pair + 1]], axis=0)
            send[side, 2 * CRIT * pair : 2 * CRIT * (pair + 1), :] = both.astype(jnp.bfloat16)

    def unpack(recv, side, ext, start):
        for pair in range(RIM // 2):
            both = recv[side, 2 * CRIT * pair : 2 * CRIT * (pair + 1), :].astype(jnp.float32)
            ext[start + 2 * pair] = both[:CRIT]
            ext[start + 2 * pair + 1] = both[CRIT:]

    for side, start in ((0, 0), (1, nblk - RIM)):
        loads[side].wait()
        for b in range(start, start + RIM):
            extend(b)
        pack(xsend, side, xcrit, RIM + start)

    pl.semaphore_wait(barrier, 1 + 2 * ncpl)

    def halo(send, recv, ssem, rsem, side):
        return pltpu.make_async_remote_copy(
            src_ref=send.at[side], dst_ref=recv.at[side], send_sem=ssem.at[side], recv_sem=rsem.at[side],
            device_id={"dom": left if side == 0 else right}, device_id_type=MESH,
        )

    def cross(src, dst, ssem, rsem, step):
        return pltpu.make_async_remote_copy(
            src_ref=src, dst_ref=dst(cpl), send_sem=ssem.at[step], recv_sem=rsem.at[cpl],
            device_id={"sec": other, "cpl": partners[step]}, device_id_type=MESH,
        )

    def arrived(src, dst, ssem, rsem, k):
        pltpu.make_async_remote_copy(
            src_ref=src, dst_ref=dst(k), send_sem=ssem.at[0], recv_sem=rsem.at[k],
            device_id={"sec": other}, device_id_type=MESH,
        ).wait_recv()

    xhalos = [halo(xsend, xrecv, xs_sem, xr_sem, side) for side in range(2)]
    yhalos = [
        pltpu.make_async_remote_copy(
            src_ref=xrest.at[pl.ds(RIM if side == 0 else nblk, RIM)],
            dst_ref=xrest.at[pl.ds(RIM + nblk if side == 0 else 0, RIM)],
            send_sem=ys_sem.at[side], recv_sem=yr_sem.at[side],
            device_id={"dom": left if side == 0 else right}, device_id_type=MESH,
        )
        for side in range(2)
    ]
    for copy in xhalos:
        copy.start()
    tabs = [cross(tab, lambda k: tab_recv.at[k], ts_sem, tr_sem, step) for step in range(ncpl)]
    for copy in tabs:
        copy.start()

    for copy in yhalos:
        copy.start()

    own_tab.wait()
    loads[2].wait()

    def extend_eight(group, carry):
        for i in range(8):
            extend(group * 8 + i)
        return carry

    lax.fori_loop(RIM // 8, (nblk - RIM) // 8, extend_eight, 0)
    loads[3].wait()
    for side in range(2):
        xhalos[side].wait_recv()
        unpack(xrecv, side, xcrit, RIM + nblk if side == 0 else 0)

    def crit_product(j, carry):
        piece = xcrit[ssrc[0, j]].astype(jnp.bfloat16)
        pcrit[j] = jnp.dot(piece, wstate[j], preferred_element_type=jnp.float32)
        return carry

    lax.fori_loop(0, tpd, crit_product, 0, unroll=True)

    def chain_crit(j, carry):
        pcrit[j] = pcrit[j] + pcrit[tab_own_s[1, j]]
        return carry

    lax.fori_loop(0, tpd, chain_crit, 0, unroll=True)
    for pair in range(tpd // 2):
        both = jnp.concatenate([pcrit[2 * pair], pcrit[2 * pair + 1]], axis=0)
        asend[2 * CRIT * pair : 2 * CRIT * (pair + 1), :] = both.astype(jnp.bfloat16)
    acopies = [cross(asend, lambda k: arecv.at[k], as_sem, ar_sem, step) for step in range(ncpl)]
    for copy in reversed(acopies):
        copy.start()

    for copy in yhalos:
        copy.wait_recv()

    def rest_product(j, carry):
        prest[j] = jnp.dot(xrest[ssrc[0, j]], wstate[j], preferred_element_type=jnp.float32)
        return carry

    lax.fori_loop(0, tpd, rest_product, 0, unroll=True)

    def chain_rest(j, carry):
        total = prest[j] + prest[tab_own_s[1, j]]
        prest[j] = total
        bsend[j] = total.astype(jnp.bfloat16)
        return carry

    lax.fori_loop(0, tpd, chain_rest, 0, unroll=True)
    bdst = lambda k: brecv.at[k, pl.ds(0, tpd)]
    bcopies = [cross(bsend, bdst, bs_sem, br_sem, 0)]
    bcopies[0].start()

    tabcopies = []
    for k in range(ncpl):
        arrived(tab, lambda k: tab_recv.at[k], ts_sem, tr_sem, k)
        copy = pltpu.make_async_copy(tab_recv.at[k], tab_s.at[k], tabcopy_sem.at[k])
        copy.start()
        tabcopies.append(copy)
    for copy in tabcopies:
        copy.wait()
    loads[5].wait()

    for k in range(ncpl):
        arrived(asend, lambda k: arecv.at[k], as_sem, ar_sem, k)
        for pair in range(tpd // 2):
            both = arecv[k, 2 * CRIT * pair : 2 * CRIT * (pair + 1), :].astype(jnp.float32)
            afull[k, 2 * pair] = both[:CRIT]
            afull[k, 2 * pair + 1] = both[CRIT:]

    first_sec = sec == 0

    def solve(group):
        for i in range(8):
            b = group * 8 + i
            got = afull[0, tab_s[0, 0, b]]
            for k in range(1, ncpl):
                got = got + afull[k, tab_s[k, 0, b]]
            at = pl.multiple_of(b * TILE, TILE)
            dout[:CRIT, pl.ds(at, TILE)] = got
            got_stage[CRIT * i : CRIT * (i + 1), :] = got
            own_stage[CRIT * i : CRIT * (i + 1), :] = xin[:CRIT, pl.ds(at, TILE)]
        atmos, ocean = [], []
        for r in range(CRIT):
            mine = own_stage[pl.ds(r, 8, stride=CRIT), :]
            got = got_stage[pl.ds(r, 8, stride=CRIT), :]
            atmos.append(jnp.where(first_sec, mine, got))
            ocean.append(jnp.where(first_sec, got, mine))
        wet_frac = wet[pl.ds(pl.multiple_of(group * 8, 8), 8), :].astype(jnp.float32)
        result = bulk_flux(atmos, ocean, wet_frac)
        for r in range(CRIT):
            got_stage[pl.ds(r, 8, stride=CRIT), :] = result[r]
        for i in range(8):
            fext[RIM + group * 8 + i] = got_stage[CRIT * i : CRIT * (i + 1), :]

    fhalos = [halo(fsend, frecv, fs_sem, fr_sem, side) for side in range(2)]
    for side, group in ((0, 0), (1, nblk // 8 - 1)):
        solve(group)
        fsend[side] = got_stage[...].astype(jnp.bfloat16)
        fhalos[side].start()

    def middle(group, carry):
        solve(group)
        return carry

    lax.fori_loop(1, nblk // 8 - 1, middle, 0)

    arrived(bsend, bdst, bs_sem, br_sem, cpl)
    for step in range(1, ncpl):
        copy = pltpu.make_async_remote_copy(
            src_ref=bdst(cpl), dst_ref=bdst(cpl), send_sem=bs_sem.at[step], recv_sem=br_sem.at[cpl],
            device_id={"cpl": partners[step]}, device_id_type=MESH,
        )
        copy.start()
        bcopies.append(copy)

    loads[4].wait()
    for side in range(2):
        fhalos[side].wait_recv()
        unpack(frecv, side, fext, RIM + nblk if side == 0 else 0)

    def flux_product(j, carry):
        piece = fext[fsrc[0, j]].astype(jnp.bfloat16)
        fbuf[j] = jnp.dot(piece, wflux[j], preferred_element_type=jnp.float32)
        return carry

    lax.fori_loop(0, tpd, flux_product, 0, unroll=True)

    def chain_flux(j, carry):
        fbuf[j] = fbuf[j] + fbuf[tab_own_s[1, j + nblk]]
        return carry

    lax.fori_loop(0, tpd, chain_flux, 0, unroll=True)
    for pair in range(tpd // 2):
        both = jnp.concatenate([fbuf[2 * pair], fbuf[2 * pair + 1]], axis=0)
        csend[2 * CRIT * pair : 2 * CRIT * (pair + 1), :] = both.astype(jnp.bfloat16)
    ccopies = [cross(csend, lambda k: crecv.at[k], cs_sem, cr_sem, step) for step in range(ncpl)]
    for copy in reversed(ccopies):
        copy.start()

    for partner in partners[1:]:
        arrived(bsend, bdst, bs_sem, br_sem, partner)

    def place(group, carry):
        for i in range(8):
            b = group * 8 + i
            got = brecv[0, tab_s[0, 0, b]].astype(jnp.float32)
            for k in range(1, ncpl):
                got = got + brecv[k, tab_s[k, 0, b]].astype(jnp.float32)
            dout[CRIT:, pl.ds(pl.multiple_of(b * TILE, TILE), TILE)] = got
        return carry

    lax.fori_loop(0, nblk // 8, place, 0)
    deliver = pltpu.make_async_copy(dout, deliv_hbm, out_sem.at[0])
    deliver.start()

    for k in range(ncpl):
        arrived(csend, lambda k: crecv.at[k], cs_sem, cr_sem, k)
        for pair in range(tpd // 2):
            both = crecv[k, 2 * CRIT * pair : 2 * CRIT * (pair + 1), :].astype(jnp.float32)
            cfull[k, 2 * pair] = both[:CRIT]
            cfull[k, 2 * pair + 1] = both[CRIT:]

    def merge(group, carry):
        wet_frac = wet[pl.ds(pl.multiple_of(group * 8, 8), 8), :].astype(jnp.float32)
        for i in range(8):
            b = group * 8 + i
            back = cfull[0, tab_s[0, 0, b + nblk]]
            for k in range(1, ncpl):
                back = back + cfull[k, tab_s[k, 0, b + nblk]]
            own = fext[RIM + b]
            fout[:, pl.ds(pl.multiple_of(b * TILE, TILE), TILE)] = 0.5 * (own + wet_frac[i : i + 1] * back)
        return carry

    lax.fori_loop(0, nblk // 8, merge, 0)
    store = pltpu.make_async_copy(fout, flux_hbm, out_sem.at[1])
    store.start()

    for copy in xhalos + yhalos + tabs + acopies + bcopies + fhalos + ccopies:
        copy.wait_send()
    deliver.wait()
    store.wait()


def settle(rows, cells, deliv_in, flux_in, deliv_out, flux_out, sems):
    half = cells // 2
    parts = [(deliv_in, deliv_out, r, h) for r in range(0, rows, CRIT) for h in (0, half)]
    parts += [(flux_in, flux_out, 0, h) for h in (0, half)]
    copies = [
        pltpu.make_async_copy(
            src.at[pl.ds(r, CRIT), pl.ds(h, half)], dst.at[0, pl.ds(r, CRIT), pl.ds(h, half)], sems.at[i]
        )
        for i, (src, dst, r, h) in enumerate(parts)
    ]
    for copy in copies:
        copy.start()
    for copy in copies:
        copy.wait()


def body(ncpl, ndom, fields, wet_mask, wstate, ssrc, stgt, wflux, fsrc, ftgt):
    rows, cells = fields.shape[1:]
    nblk = cells // TILE
    tpd = wstate.shape[1]
    rest = rows - CRIT
    f32, bf16, i32 = jnp.float32, jnp.bfloat16, jnp.int32
    vmem, dma = pltpu.VMEM, pltpu.SemaphoreType.DMA
    hbm_spec = pl.BlockSpec(memory_space=pltpu.HBM)
    delivered, fluxes = pl.pallas_call(
        functools.partial(kernel, (rows, nblk, tpd, ncpl, ndom)),
        out_shape=(
            jax.ShapeDtypeStruct((rows, cells), f32),
            jax.ShapeDtypeStruct((CRIT, cells), f32),
        ),
        in_specs=[hbm_spec] * 8,
        out_specs=(hbm_spec, hbm_spec),
        scratch_shapes=[pltpu.SMEM((1, tpd), i32)] * 4
        + [
            vmem((rows, cells), f32),
            vmem((nblk + 2 * RIM, CRIT, TILE), f32),
            vmem((nblk + 2 * RIM, rest, TILE), bf16),
            vmem((nblk, TILE), i32),
            vmem((tpd, TILE, TILE), bf16),
            vmem((tpd, TILE, TILE), bf16),
            vmem((tpd + 1, CRIT, TILE), f32),
            vmem((tpd + 1, rest, TILE), f32),
            vmem((tpd + 1, CRIT, TILE), f32),
            vmem((nblk + 2 * RIM, CRIT, TILE), f32),
            vmem((rows, cells), f32),
            vmem((CRIT, cells), f32),
            vmem((8 * CRIT, TILE), f32),
            vmem((8 * CRIT, TILE), f32),
            vmem((2, RIM * CRIT, TILE), bf16),
            vmem((2, RIM * CRIT, TILE), bf16),
            vmem((2, RIM * CRIT, TILE), bf16),
            vmem((2, RIM * CRIT, TILE), bf16),
            vmem((8, 2 * nblk), i32),
            vmem((ncpl, 8, 2 * nblk), i32),
            pltpu.SMEM((8, 2 * nblk), i32),
            pltpu.SMEM((ncpl, 8, 2 * nblk), i32),
            vmem((tpd * CRIT, TILE), bf16),
            vmem((ncpl, tpd * CRIT, TILE), bf16),
            vmem((tpd, rest, TILE), bf16),
            vmem((ncpl, tpd + 1, rest, TILE), bf16),
            vmem((tpd * CRIT, TILE), bf16),
            vmem((ncpl, tpd * CRIT, TILE), bf16),
            vmem((ncpl, tpd + 1, CRIT, TILE), f32),
            vmem((ncpl, tpd + 1, CRIT, TILE), f32),
            dma((10,)), dma((ncpl + 1,)), dma((2,)),
            dma((2,)), dma((2,)), dma((2,)), dma((2,)), dma((2,)), dma((2,)),
            dma((ncpl,)), dma((ncpl,)), dma((ncpl,)), dma((ncpl,)),
            dma((ncpl,)), dma((ncpl,)), dma((ncpl,)), dma((ncpl,)),
        ],
        compiler_params=pltpu.CompilerParams(
            collective_id=0, has_side_effects=True, vmem_limit_bytes=63 * 1024 * 1024
        ),
    )(ssrc, stgt, fsrc, ftgt, fields, wet_mask.reshape(nblk, TILE), wstate, wflux)
    return pl.pallas_call(
        functools.partial(settle, rows, cells),
        out_shape=(
            jax.ShapeDtypeStruct((1, rows, cells), f32),
            jax.ShapeDtypeStruct((1, CRIT, cells), f32),
        ),
        in_specs=[hbm_spec] * 2,
        out_specs=(hbm_spec, hbm_spec),
        scratch_shapes=[dma((2 * (rows // CRIT + 1),))],
    )(delivered, fluxes)


def solution(mesh):
    tile_spec = P("sec", ("cpl", "dom"), None, None)
    index_spec = P("sec", ("cpl", "dom"))
    return jax.shard_map(
        functools.partial(body, mesh.shape["cpl"], mesh.shape["dom"]),
        mesh=mesh,
        in_specs=(
            P("sec", None, "dom"), P("sec", "dom"),
            tile_spec, index_spec, index_spec,
            tile_spec, index_spec, index_spec,
        ),
        out_specs=(P("sec", None, "dom"), P("sec", None, "dom")),
        check_vma=False,
    )
```

```python
import functools

import jax
import jax.numpy as jnp
from jax import lax
from jax.experimental import pallas as pl
from jax.experimental.pallas import tpu as pltpu
from jax.sharding import PartitionSpec as P

TILE = 128
BULK_ITERS = 3
RIM = 8
CRIT = 8
MESH = pl.DeviceIdType.MESH


def bulk_flux(atmos, ocean, wet_frac):
    wind_u = atmos[0] - ocean[0]
    wind_v = atmos[1] - ocean[1]
    square = wind_u * wind_u + wind_v * wind_v + 0.5
    wind_speed = jnp.sqrt(square)
    temp_diff = atmos[2] - ocean[2]
    humid_diff = atmos[3] - 0.5 * ocean[3]
    neutral = 1.0 + 0.5 * jnp.tanh(atmos[4] + ocean[4])
    richardson = 2.0 * temp_diff / square
    drag_coef = neutral
    for _ in range(BULK_ITERS):
        drag_coef = neutral * (1.0 + 0.8 * jnp.tanh(-richardson * drag_coef))
    transfer = drag_coef * wind_speed
    rows = [
        0.5 * transfer * wind_u,
        0.5 * transfer * wind_v,
        0.5 * transfer * temp_diff,
        0.5 * transfer * humid_diff,
        atmos[5] * (1.0 - 0.3 * jnp.tanh(ocean[5])),
        atmos[6] - 0.5 * ocean[2],
        atmos[7] - 0.15 * transfer * humid_diff,
        0.5 * jnp.sqrt(drag_coef) * wind_speed,
    ]
    return [row * wet_frac for row in rows]


def kernel(
    sizes,
    ssrc_hbm, stgt_hbm, fsrc_hbm, ftgt_hbm,
    fields_hbm, wet_hbm, wstate_hbm, wflux_hbm,
    dout, fout,
    ssrc, stgt, fsrc, ftgt,
    xin, xcrit, xrest, wet, wstate, wflux, pcrit, prest, fbuf, fext, own_stage, got_stage,
    xsend, xrecv, fsend, frecv,
    tab, tab_recv, tab_own_s, tab_s,
    asend, arecv, bsend, brecv, csend, crecv, afull, cfull,
    load_sem, tabcopy_sem,
    xs_sem, xr_sem, ys_sem, yr_sem, fs_sem, fr_sem,
    ts_sem, tr_sem, as_sem, ar_sem, bs_sem, br_sem, cs_sem, cr_sem,
):
    rows, nblk, tpd, ncpl, ndom = sizes
    rest = rows - CRIT
    edge = RIM * TILE
    cells = nblk * TILE
    sec = lax.axis_index("sec")
    cpl = lax.axis_index("cpl")
    dom = lax.axis_index("dom")
    right = lax.rem(dom + 1, ndom)
    left = lax.rem(dom + ndom - 1, ndom)
    other = 1 - sec

    indices = [
        pltpu.make_async_copy(src, dst, load_sem.at[6 + i])
        for i, (src, dst) in enumerate(((stgt_hbm, stgt), (ftgt_hbm, ftgt), (ssrc_hbm, ssrc), (fsrc_hbm, fsrc)))
    ]
    for load in indices:
        load.start()
    loads = [
        pltpu.make_async_copy(fields_hbm.at[0, :, pl.ds(0, edge)], xin.at[:, pl.ds(0, edge)], load_sem.at[0]),
        pltpu.make_async_copy(fields_hbm.at[0, :, pl.ds(cells - edge, edge)], xin.at[:, pl.ds(cells - edge, edge)], load_sem.at[1]),
        pltpu.make_async_copy(fields_hbm.at[0, :, pl.ds(edge, cells - 2 * edge)], xin.at[:, pl.ds(edge, cells - 2 * edge)], load_sem.at[2]),
        pltpu.make_async_copy(wstate_hbm.at[0], wstate, load_sem.at[3]),
        pltpu.make_async_copy(wflux_hbm.at[0], wflux, load_sem.at[4]),
        pltpu.make_async_copy(wet_hbm, wet, load_sem.at[5]),
    ]
    for load in loads:
        load.start()

    barrier = pltpu.get_barrier_semaphore()
    for neighbour in (left, right):
        pl.semaphore_signal(barrier, inc=1, device_id={"dom": neighbour}, device_id_type=MESH)
    partners = [lax.rem(cpl + step, ncpl) for step in range(ncpl)]
    for partner in partners:
        pl.semaphore_signal(barrier, inc=1, device_id={"sec": other, "cpl": partner}, device_id_type=MESH)
    for partner in partners[1:]:
        pl.semaphore_signal(barrier, inc=1, device_id={"cpl": partner}, device_id_type=MESH)

    lane = lax.broadcasted_iota(jnp.int32, (8, 2 * nblk), 1)
    sub = lax.broadcasted_iota(jnp.int32, (8, 2 * nblk), 0)
    last = jnp.full((8, 2 * nblk), tpd, jnp.int32)
    prev = jnp.full((8, 2 * nblk), tpd, jnp.int32)
    trow = jnp.full((8, 2 * nblk), -1, jnp.int32)

    for load in indices:
        load.wait()

    def mark(j, carry):
        last, trow = carry
        a = stgt[0, j]
        b = ftgt[0, j] + nblk
        last = jnp.where((lane == a) | (lane == b), j, last)
        trow = jnp.where(lane == j, a, trow)
        trow = jnp.where(lane == j + nblk, b, trow)
        return last, trow

    last, trow = lax.fori_loop(0, tpd, mark, (last, trow), unroll=True)

    def link(j, prev):
        a = stgt[0, j]
        b = ftgt[0, j] + nblk
        prev = jnp.where((trow == a) & (lane > j), j, prev)
        return jnp.where((trow == b) & (lane > j + nblk), j, prev)

    prev = lax.fori_loop(0, tpd, link, prev, unroll=True)
    tab[...] = jnp.where(sub == 0, last, prev)
    own_tab = pltpu.make_async_copy(tab, tab_own_s, tabcopy_sem.at[ncpl])
    own_tab.start()

    pcrit[tpd] = jnp.zeros((CRIT, TILE), jnp.float32)
    prest[tpd] = jnp.zeros((rest, TILE), jnp.float32)
    fbuf[tpd] = jnp.zeros((CRIT, TILE), jnp.float32)
    for k in range(ncpl):
        afull[k, tpd] = jnp.zeros((CRIT, TILE), jnp.float32)
        cfull[k, tpd] = jnp.zeros((CRIT, TILE), jnp.float32)
        brecv[k, tpd] = jnp.zeros((rest, TILE), jnp.bfloat16)

    def extend(b):
        at = b * TILE if isinstance(b, int) else pl.multiple_of(b * TILE, TILE)
        xcrit[RIM + b] = xin[:CRIT, pl.ds(at, TILE)]
        xrest[RIM + b] = xin[CRIT:, pl.ds(at, TILE)].astype(jnp.bfloat16)

    def pack(send, side, ext, start):
        for pair in range(RIM // 2):
            both = jnp.concatenate([ext[start + 2 * pair], ext[start + 2 * pair + 1]], axis=0)
            send[side, 2 * CRIT * pair : 2 * CRIT * (pair + 1), :] = both.astype(jnp.bfloat16)

    def unpack(recv, side, ext, start):
        for pair in range(RIM // 2):
            both = recv[side, 2 * CRIT * pair : 2 * CRIT * (pair + 1), :].astype(jnp.float32)
            ext[start + 2 * pair] = both[:CRIT]
            ext[start + 2 * pair + 1] = both[CRIT:]

    for side, start in ((0, 0), (1, nblk - RIM)):
        loads[side].wait()
        for b in range(start, start + RIM):
            extend(b)
        pack(xsend, side, xcrit, RIM + start)

    pl.semaphore_wait(barrier, 1 + 2 * ncpl)

    def halo(send, recv, ssem, rsem, side):
        return pltpu.make_async_remote_copy(
            src_ref=send.at[side], dst_ref=recv.at[side], send_sem=ssem.at[side], recv_sem=rsem.at[side],
            device_id={"dom": left if side == 0 else right}, device_id_type=MESH,
        )

    def cross(src, dst, ssem, rsem, step):
        return pltpu.make_async_remote_copy(
            src_ref=src, dst_ref=dst(cpl), send_sem=ssem.at[step], recv_sem=rsem.at[cpl],
            device_id={"sec": other, "cpl": partners[step]}, device_id_type=MESH,
        )

    def arrived(src, dst, ssem, rsem, k):
        pltpu.make_async_remote_copy(
            src_ref=src, dst_ref=dst(k), send_sem=ssem.at[0], recv_sem=rsem.at[k],
            device_id={"sec": other}, device_id_type=MESH,
        ).wait_recv()

    xhalos = [halo(xsend, xrecv, xs_sem, xr_sem, side) for side in range(2)]
    yhalos = [
        pltpu.make_async_remote_copy(
            src_ref=xrest.at[pl.ds(RIM if side == 0 else nblk, RIM)],
            dst_ref=xrest.at[pl.ds(RIM + nblk if side == 0 else 0, RIM)],
            send_sem=ys_sem.at[side], recv_sem=yr_sem.at[side],
            device_id={"dom": left if side == 0 else right}, device_id_type=MESH,
        )
        for side in range(2)
    ]
    for copy in xhalos:
        copy.start()
    tabs = [cross(tab, lambda k: tab_recv.at[k], ts_sem, tr_sem, step) for step in range(ncpl)]
    for copy in tabs:
        copy.start()

    for copy in yhalos:
        copy.start()

    own_tab.wait()
    loads[2].wait()

    def extend_eight(group, carry):
        for i in range(8):
            extend(group * 8 + i)
        return carry

    lax.fori_loop(RIM // 8, (nblk - RIM) // 8, extend_eight, 0)
    loads[3].wait()
    for side in range(2):
        xhalos[side].wait_recv()
        unpack(xrecv, side, xcrit, RIM + nblk if side == 0 else 0)

    def crit_product(j, carry):
        piece = xcrit[ssrc[0, j]].astype(jnp.bfloat16)
        pcrit[j] = jnp.dot(piece, wstate[j], preferred_element_type=jnp.float32)
        return carry

    lax.fori_loop(0, tpd, crit_product, 0, unroll=True)

    def chain_crit(j, carry):
        pcrit[j] = pcrit[j] + pcrit[tab_own_s[1, j]]
        return carry

    lax.fori_loop(0, tpd, chain_crit, 0, unroll=True)
    for pair in range(tpd // 2):
        both = jnp.concatenate([pcrit[2 * pair], pcrit[2 * pair + 1]], axis=0)
        asend[2 * CRIT * pair : 2 * CRIT * (pair + 1), :] = both.astype(jnp.bfloat16)
    acopies = [cross(asend, lambda k: arecv.at[k], as_sem, ar_sem, step) for step in range(ncpl)]
    for copy in reversed(acopies):
        copy.start()

    for copy in yhalos:
        copy.wait_recv()

    def rest_product(j, carry):
        prest[j] = jnp.dot(xrest[ssrc[0, j]], wstate[j], preferred_element_type=jnp.float32)
        return carry

    lax.fori_loop(0, tpd, rest_product, 0, unroll=True)

    def chain_rest(j, carry):
        total = prest[j] + prest[tab_own_s[1, j]]
        prest[j] = total
        bsend[j] = total.astype(jnp.bfloat16)
        return carry

    lax.fori_loop(0, tpd, chain_rest, 0, unroll=True)
    bdst = lambda k: brecv.at[k, pl.ds(0, tpd)]
    bcopies = [cross(bsend, bdst, bs_sem, br_sem, 0)]
    bcopies[0].start()

    tabcopies = []
    for k in range(ncpl):
        arrived(tab, lambda k: tab_recv.at[k], ts_sem, tr_sem, k)
        copy = pltpu.make_async_copy(tab_recv.at[k], tab_s.at[k], tabcopy_sem.at[k])
        copy.start()
        tabcopies.append(copy)
    for copy in tabcopies:
        copy.wait()
    loads[5].wait()

    for k in range(ncpl):
        arrived(asend, lambda k: arecv.at[k], as_sem, ar_sem, k)
        for pair in range(tpd // 2):
            both = arecv[k, 2 * CRIT * pair : 2 * CRIT * (pair + 1), :].astype(jnp.float32)
            afull[k, 2 * pair] = both[:CRIT]
            afull[k, 2 * pair + 1] = both[CRIT:]

    first_sec = sec == 0

    def solve(group):
        for i in range(8):
            b = group * 8 + i
            got = afull[0, tab_s[0, 0, b]]
            for k in range(1, ncpl):
                got = got + afull[k, tab_s[k, 0, b]]
            at = pl.multiple_of(b * TILE, TILE)
            dout[:CRIT, pl.ds(at, TILE)] = got
            got_stage[CRIT * i : CRIT * (i + 1), :] = got
            own_stage[CRIT * i : CRIT * (i + 1), :] = xin[:CRIT, pl.ds(at, TILE)]
        atmos, ocean = [], []
        for r in range(CRIT):
            mine = own_stage[pl.ds(r, 8, stride=CRIT), :]
            got = got_stage[pl.ds(r, 8, stride=CRIT), :]
            atmos.append(jnp.where(first_sec, mine, got))
            ocean.append(jnp.where(first_sec, got, mine))
        wet_frac = wet[pl.ds(pl.multiple_of(group * 8, 8), 8), :].astype(jnp.float32)
        result = bulk_flux(atmos, ocean, wet_frac)
        for r in range(CRIT):
            got_stage[pl.ds(r, 8, stride=CRIT), :] = result[r]
        for i in range(8):
            fext[RIM + group * 8 + i] = got_stage[CRIT * i : CRIT * (i + 1), :]

    fhalos = [halo(fsend, frecv, fs_sem, fr_sem, side) for side in range(2)]
    for side, group in ((0, 0), (1, nblk // 8 - 1)):
        solve(group)
        fsend[side] = got_stage[...].astype(jnp.bfloat16)
        fhalos[side].start()

    def middle(group, carry):
        solve(group)
        return carry

    lax.fori_loop(1, nblk // 8 - 1, middle, 0)

    arrived(bsend, bdst, bs_sem, br_sem, cpl)
    for step in range(1, ncpl):
        copy = pltpu.make_async_remote_copy(
            src_ref=bdst(cpl), dst_ref=bdst(cpl), send_sem=bs_sem.at[step], recv_sem=br_sem.at[cpl],
            device_id={"cpl": partners[step]}, device_id_type=MESH,
        )
        copy.start()
        bcopies.append(copy)

    loads[4].wait()
    for side in range(2):
        fhalos[side].wait_recv()
        unpack(frecv, side, fext, RIM + nblk if side == 0 else 0)

    def flux_product(j, carry):
        piece = fext[fsrc[0, j]].astype(jnp.bfloat16)
        fbuf[j] = jnp.dot(piece, wflux[j], preferred_element_type=jnp.float32)
        return carry

    lax.fori_loop(0, tpd, flux_product, 0, unroll=True)

    def chain_flux(j, carry):
        fbuf[j] = fbuf[j] + fbuf[tab_own_s[1, j + nblk]]
        return carry

    lax.fori_loop(0, tpd, chain_flux, 0, unroll=True)
    for pair in range(tpd // 2):
        both = jnp.concatenate([fbuf[2 * pair], fbuf[2 * pair + 1]], axis=0)
        csend[2 * CRIT * pair : 2 * CRIT * (pair + 1), :] = both.astype(jnp.bfloat16)
    ccopies = [cross(csend, lambda k: crecv.at[k], cs_sem, cr_sem, step) for step in range(ncpl)]
    for copy in reversed(ccopies):
        copy.start()

    for partner in partners[1:]:
        arrived(bsend, bdst, bs_sem, br_sem, partner)

    def place(group, carry):
        for i in range(8):
            b = group * 8 + i
            got = brecv[0, tab_s[0, 0, b]].astype(jnp.float32)
            for k in range(1, ncpl):
                got = got + brecv[k, tab_s[k, 0, b]].astype(jnp.float32)
            dout[CRIT:, pl.ds(pl.multiple_of(b * TILE, TILE), TILE)] = got
        return carry

    lax.fori_loop(0, nblk // 8, place, 0)

    for k in range(ncpl):
        arrived(csend, lambda k: crecv.at[k], cs_sem, cr_sem, k)
        for pair in range(tpd // 2):
            both = crecv[k, 2 * CRIT * pair : 2 * CRIT * (pair + 1), :].astype(jnp.float32)
            cfull[k, 2 * pair] = both[:CRIT]
            cfull[k, 2 * pair + 1] = both[CRIT:]

    def merge(group, carry):
        wet_frac = wet[pl.ds(pl.multiple_of(group * 8, 8), 8), :].astype(jnp.float32)
        for i in range(8):
            b = group * 8 + i
            back = cfull[0, tab_s[0, 0, b + nblk]]
            for k in range(1, ncpl):
                back = back + cfull[k, tab_s[k, 0, b + nblk]]
            own = fext[RIM + b]
            fout[:, pl.ds(pl.multiple_of(b * TILE, TILE), TILE)] = 0.5 * (own + wet_frac[i : i + 1] * back)
        return carry

    lax.fori_loop(0, nblk // 8, merge, 0)

    for copy in xhalos + yhalos + tabs + acopies + bcopies + fhalos + ccopies:
        copy.wait_send()


def settle(rows, cells, deliv_in, flux_in, deliv_out, flux_out, sems):
    half = cells // 2
    parts = [(deliv_in, deliv_out, r, h) for r in range(0, rows, CRIT) for h in (0, half)]
    parts += [(flux_in, flux_out, 0, h) for h in (0, half)]
    copies = [
        pltpu.make_async_copy(
            src.at[pl.ds(r, CRIT), pl.ds(h, half)], dst.at[0, pl.ds(r, CRIT), pl.ds(h, half)], sems.at[i]
        )
        for i, (src, dst, r, h) in enumerate(parts)
    ]
    for copy in copies:
        copy.start()
    for copy in copies:
        copy.wait()


def body(ncpl, ndom, fields, wet_mask, wstate, ssrc, stgt, wflux, fsrc, ftgt):
    rows, cells = fields.shape[1:]
    nblk = cells // TILE
    tpd = wstate.shape[1]
    rest = rows - CRIT
    f32, bf16, i32 = jnp.float32, jnp.bfloat16, jnp.int32
    vmem, dma = pltpu.VMEM, pltpu.SemaphoreType.DMA
    hbm_spec = pl.BlockSpec(memory_space=pltpu.HBM)
    vmem_spec = pl.BlockSpec(memory_space=pltpu.VMEM)
    delivered, fluxes = pl.pallas_call(
        functools.partial(kernel, (rows, nblk, tpd, ncpl, ndom)),
        out_shape=(
            pltpu.VMEM((rows, cells), f32),
            pltpu.VMEM((CRIT, cells), f32),
        ),
        in_specs=[hbm_spec] * 8,
        out_specs=(vmem_spec, vmem_spec),
        scratch_shapes=[pltpu.SMEM((1, tpd), i32)] * 4
        + [
            vmem((rows, cells), f32),
            vmem((nblk + 2 * RIM, CRIT, TILE), f32),
            vmem((nblk + 2 * RIM, rest, TILE), bf16),
            vmem((nblk, TILE), i32),
            vmem((tpd, TILE, TILE), bf16),
            vmem((tpd, TILE, TILE), bf16),
            vmem((tpd + 1, CRIT, TILE), f32),
            vmem((tpd + 1, rest, TILE), f32),
            vmem((tpd + 1, CRIT, TILE), f32),
            vmem((nblk + 2 * RIM, CRIT, TILE), f32),
            vmem((8 * CRIT, TILE), f32),
            vmem((8 * CRIT, TILE), f32),
            vmem((2, RIM * CRIT, TILE), bf16),
            vmem((2, RIM * CRIT, TILE), bf16),
            vmem((2, RIM * CRIT, TILE), bf16),
            vmem((2, RIM * CRIT, TILE), bf16),
            vmem((8, 2 * nblk), i32),
            vmem((ncpl, 8, 2 * nblk), i32),
            pltpu.SMEM((8, 2 * nblk), i32),
            pltpu.SMEM((ncpl, 8, 2 * nblk), i32),
            vmem((tpd * CRIT, TILE), bf16),
            vmem((ncpl, tpd * CRIT, TILE), bf16),
            vmem((tpd, rest, TILE), bf16),
            vmem((ncpl, tpd + 1, rest, TILE), bf16),
            vmem((tpd * CRIT, TILE), bf16),
            vmem((ncpl, tpd * CRIT, TILE), bf16),
            vmem((ncpl, tpd + 1, CRIT, TILE), f32),
            vmem((ncpl, tpd + 1, CRIT, TILE), f32),
            dma((10,)), dma((ncpl + 1,)),
            dma((2,)), dma((2,)), dma((2,)), dma((2,)), dma((2,)), dma((2,)),
            dma((ncpl,)), dma((ncpl,)), dma((ncpl,)), dma((ncpl,)),
            dma((ncpl,)), dma((ncpl,)), dma((ncpl,)), dma((ncpl,)),
        ],
        compiler_params=pltpu.CompilerParams(
            collective_id=0, has_side_effects=True, vmem_limit_bytes=61 * 1024 * 1024
        ),
    )(ssrc, stgt, fsrc, ftgt, fields, wet_mask.reshape(nblk, TILE), wstate, wflux)
    return pl.pallas_call(
        functools.partial(settle, rows, cells),
        out_shape=(
            jax.ShapeDtypeStruct((1, rows, cells), f32),
            jax.ShapeDtypeStruct((1, CRIT, cells), f32),
        ),
        in_specs=[pl.BlockSpec(memory_space=pl.ANY)] * 2,
        out_specs=(hbm_spec, hbm_spec),
        scratch_shapes=[dma((2 * (rows // CRIT + 1),))],
        compiler_params=pltpu.CompilerParams(vmem_limit_bytes=4 * 1024 * 1024),
    )(delivered, fluxes)


def solution(mesh):
    tile_spec = P("sec", ("cpl", "dom"), None, None)
    index_spec = P("sec", ("cpl", "dom"))
    return jax.shard_map(
        functools.partial(body, mesh.shape["cpl"], mesh.shape["dom"]),
        mesh=mesh,
        in_specs=(
            P("sec", None, "dom"), P("sec", "dom"),
            tile_spec, index_spec, index_spec,
            tile_spec, index_spec, index_spec,
        ),
        out_specs=(P("sec", None, "dom"), P("sec", None, "dom")),
        check_vma=False,
    )
```
